32 devices in a mesh: req: 8 (over z, x), mlp: 4 (over y, core).
Axes of the slice: x: 2, y: 2, z: 4, core: 2. Of those that a mesh axis runs over, the one named last changes fastest.
Arguments:
- tokens: bfloat16 [4096, 4096], P('req'), may hold values from -16 to 16
- grid_sides: int32 [16, 2], P('req'), may hold values from 10 to 14, as said below
- offsets: int32 [16], P('req'), may hold values from 0 to 201, as said below
- merge_rows: int32 [1024, 4], P('req'), may hold values from 0 to 401, as said below
- routes: int32 [1024, 1], replicated, may hold values from 0 to 7; in each aligned block of 128 rows (0 to 127, 128 to 255, ...) at most 16 rows name the same one
- norm_gain: float32 [2, 4096], replicated, may hold values from 0.5 to 1.5
- norm_bias: float32 [2, 4096], replicated, may hold values from -1.5 to 1.5
- layer_scale: float32 [2, 4096], replicated, may hold values from 0.2 to 1
- qkv_weight: bfloat16 [4096, 6144], P('req', 'mlp'), may hold values from -2.34375 to 2.34375
- out_weight: bfloat16 [2048, 4096], P('mlp', 'req'), may hold values from -0.125 to 0.125
- gate_up: bfloat16 [2, 4096, 4096], P(None, 'req', 'mlp'), may hold values from -0.09375 to 0.09375
- down_weight: bfloat16 [4096, 4096], P('mlp', 'req'), may hold values from -0.09375 to 0.09375
- merge_gain: float32 [4, 4096], P(None, 'mlp'), may hold values from 0.5 to 1.5
- merge_bias: float32 [4, 4096], P(None, 'mlp'), may hold values from -1.5 to 1.5
- merge_weight: bfloat16 [4, 4096, 2048], P(None, 'mlp', 'req'), may hold values from -0.1875 to 0.1875
Outputs:
- embeds: bfloat16 [1024, 2048], P('req', 'mlp')
- token_norms: float32 [1024], P('req')
- max_logits: float32 [16, 16], P('req', 'mlp')
The draws below stay inside these ranges and needn't reach their ends.
Inputs may be any that keep to these rules, and one draw needn't show every extreme that they name: `grid_sides`: sides are even; the first 2 of all 16 images are 14 x 14 and the last image is 10 x 10. `offsets`: the images of a group are packed in order from in-group row 0: image g * 2 + j starts at the sum of 5 + h w over images g * 2 to g * 2 + j - 1. `merge_rows`: for slot k of group g, image i = g * 2 + k div 64 of grid h x w at offset o and m = k mod 64: if m < (h / 2)(w / 2), the entries are o + 5 + (2 a + e) w + 2 b + f for (e, f) = (0, 0), (0, 1), (1, 0), (1, 1), with a = m div (w / 2), b = m mod (w / 2); otherwise all four are 0. `routes`: among the 128 slots of one group, no value appears more than 16 times.
All inputs are finite; a program needn't handle non-finite values.
Results may differ from the reference program's by a relative error of at most 0.017.
Values may be sent and summed in bfloat16 or wider, within the bound.
A program may use at most 128 MiB of HBM per device.

```python
import math
import jax
import jax.numpy as jnp
import numpy as np
from jax import lax

D = 4096
HEADS = 16
HEAD = 128
HID = 4096
OUT = 2048
GMIN = 10
GMAX = 14
IPG = 2
MSLOT = 64
ROWS = 512
MG = 128
CAP = 16
ROUTED = 128
IMAGES = 16
N_REQ = 8
N_MLP = 4


def grid_values(key):
    sub_key = jax.random.fold_in(key, 11)
    levels = (GMAX - GMIN) // 2 + 1
    grid_vals = jax.random.randint(sub_key, (IMAGES, 2), 0, levels) * 2 + GMIN
    image_ids = jnp.arange(IMAGES, dtype=jnp.int32)
    leading = IPG
    grid_vals = jnp.where((image_ids < leading)[:, None], GMAX, grid_vals)
    grid_vals = grid_vals.at[IMAGES - 1].set(GMIN)
    return grid_vals.astype(jnp.int32)


def packed_starts(grid_vals):
    lengths = 5 + grid_vals[:, 0] * grid_vals[:, 1]
    per_group = lengths.reshape(IMAGES // IPG, IPG)
    return (jnp.cumsum(per_group, axis=1) - per_group).reshape(IMAGES).astype(jnp.int32)


def draw_grid_sides(key, part):
    return grid_values(key)


def draw_offsets(key, part):
    return packed_starts(grid_values(key))


def draw_merge_rows(key, part):
    grid_vals = grid_values(key)
    starts = packed_starts(grid_vals)
    groups = IMAGES // IPG
    slot_ids = jnp.arange(IPG * MSLOT, dtype=jnp.int32)
    local_image = slot_ids // MSLOT
    within = slot_ids % MSLOT
    image_ids = jnp.arange(groups, dtype=jnp.int32)[:, None] * IPG + local_image[None, :]
    height = grid_vals[image_ids, 0]
    breadth = grid_vals[image_ids, 1]
    anchor = starts[image_ids]
    half_width = breadth // 2
    row_pair = within[None, :] // half_width
    col_pair = within[None, :] % half_width
    is_live = within[None, :] < height // 2 * half_width
    first_row = anchor + 5 + 2 * row_pair * breadth + 2 * col_pair
    picked = jnp.stack([first_row, first_row + 1, first_row + breadth, first_row + breadth + 1], axis=-1)
    picked = jnp.where(is_live[..., None], picked, 0)
    return picked.reshape(groups * IPG * MSLOT, 4).astype(jnp.int32)


def draw_tokens(key, part):
    key_a, key_b = jax.random.split(key, 2)
    total_rows = IMAGES // IPG * ROWS
    column = jnp.arange(D, dtype=jnp.float32) / D
    rough = jnp.exp(jax.random.uniform(key_b, (D,), minval=-0.35, maxval=0.35))
    col_scale = 0.6 * 3.0 ** column * rough
    drawn = jnp.clip(jax.random.normal(key_a, (total_rows, D)), -6.0, 6.0) * col_scale[None, :]
    return drawn.astype(jnp.bfloat16)


def draw_qkv_weight(key, part):
    key_a = jax.random.fold_in(key, 0)
    drawn = jnp.clip(jax.random.normal(key_a, (D, HEADS, 3, HEAD)), -6.0, 6.0) / math.sqrt(D)
    return drawn.reshape(D, HEADS * 3 * HEAD).astype(jnp.bfloat16)


def draw_merge_weight(key, part):
    key_a, key_b = jax.random.split(key, 2)
    col_scale = jnp.exp(jax.random.uniform(key_b, (OUT,), minval=math.log(0.4), maxval=math.log(2.5)))
    drawn = jnp.clip(jax.random.normal(key_a, (4, D, OUT)), -6.0, 6.0)
    return (drawn * col_scale[None, None, :] / math.sqrt(4 * D)).astype(jnp.bfloat16)


def steps_of(key, shape, cuts, least, high):
    loudness, own = 1.0, jax.random.fold_in(key, 6)
    for dim, blocks in cuts:
        steps = jnp.exp(jax.random.uniform(jax.random.fold_in(own, dim), (blocks,), jnp.float32, least / len(cuts), high / len(cuts)))
        loudness = loudness * jnp.repeat(steps, shape[dim] // blocks).reshape([-1 if axis == dim else 1 for axis in range(len(shape))])
    return loudness


def deal_out(rng, own, number, rows, amount, top, most, skew):
    ranking = jax.random.permutation(rng, amount)
    crowded, common = load_shares(amount, rows * top, most, skew, True), load_shares(amount, rows * top, most, skew, False)
    places = jnp.arange(amount)

    def named(tallies, offset_by):
        used = int((tallies > 0).sum())
        fixed = max(1, used // 4)
        passed = fixed + (places - fixed + offset_by * (used - fixed)) % max(1, amount - fixed)
        return jnp.zeros((amount,), jnp.int32).at[ranking[jnp.where(places < fixed, places, passed)]].set(jnp.asarray(tallies, jnp.int32))

    tallies = jnp.where(number % 4 == 0, named(crowded, number // 4), named(common, number - number // 4 - 1))
    mixed = jax.random.permutation(jax.random.fold_in(own, 3), amount)
    source_of, taker = mixed[0:amount // 2 * 2:2], mixed[1:amount // 2 * 2:2]
    margin = jnp.minimum(tallies[source_of] - 1, most - tallies[taker]) // 2
    margin = jnp.where((source_of == ranking[0]) | (taker == ranking[0]) | (tallies[taker] == 0), 0, jnp.maximum(margin, 0))
    passed = jax.random.randint(jax.random.fold_in(own, 4), (amount // 2,), 0, 1 << 20) % (margin + 1)
    tallies = tallies.at[source_of].add(-passed).at[taker].add(passed)
    members = jnp.searchsorted(jnp.cumsum(tallies), jnp.arange(rows * top), side="right").astype(jnp.int32)
    grid = members.reshape(top, rows).T
    grid = grid[jax.random.permutation(jax.random.fold_in(own, 1), rows)]
    offset_by = jax.random.randint(jax.random.fold_in(own, 2), (rows, 1), 0, top)
    return jnp.take_along_axis(grid, (jnp.arange(top)[None, :] + offset_by) % top, axis=1)


def load_shares(amount, total, limit, skew, full):
    weights = [(1 << 20) // math.isqrt(rank ** skew) + 1 for rank in range(1, amount + 1)]
    largest = limit if full else min(limit, max(-(-total // amount), total * weights[0] // sum(weights)))
    least = 1 if total - largest >= amount - 1 else 0
    holding, surplus = [largest] + [least] * (amount - 1), total - largest - least * (amount - 1)
    while surplus > 0:
        movable = [i for i in range(1, amount) if holding[i] < largest] or [i for i in range(1, amount) if holding[i] < limit]
        whole, remaining = sum([weights[i] for i in movable]), surplus
        for i in movable:
            addition = min(limit - holding[i], max(1, remaining * weights[i] // whole), surplus)
            holding[i] = holding[i] + addition
            surplus = surplus - addition
    return np.array(holding)


def gaussian(stream_key, extent, deviation, limit, cuts=(), kind=jnp.bfloat16):
    values = deviation * jax.random.normal(stream_key, extent, jnp.float32)
    if cuts:
        values = values * steps_of(stream_key, extent, cuts, -0.22, 0.18)
    return jnp.clip(values, -limit, limit).astype(kind)


def setup_inputs(seed: int = 0) -> dict:
    keys = jax.random.split(jax.random.key(seed), 16)
    tokens = draw_tokens(jax.random.fold_in(keys[15], 71), 0)
    grid_sides = draw_grid_sides(jax.random.fold_in(keys[15], 71), 0)
    offsets = draw_offsets(jax.random.fold_in(keys[15], 71), 0)
    merge_rows = draw_merge_rows(jax.random.fold_in(keys[15], 71), 0)
    routes_keys = jax.random.split(jax.random.fold_in(keys[4], 1), (N_REQ * MG) // MG)
    routes_turns = jax.random.permutation(jax.random.fold_in(keys[4], 3), (N_REQ * MG) // MG)
    routes = jax.vmap(lambda own, number: deal_out(jax.random.fold_in(keys[4], 2), own, number, MG, N_REQ, 1, CAP, 2))(routes_keys, routes_turns).reshape((N_REQ * MG, 1))
    norm_gain = jnp.clip(1.0 + 0.1 * jax.random.normal(keys[5], (2, D), jnp.float32), 0.5, 1.5)
    norm_bias = gaussian(keys[6], (2, D), 0.3, 1.5, (), jnp.float32)
    layer_scale = jnp.clip(jnp.exp(jax.random.uniform(keys[7], (2, D), jnp.float32, math.log(0.2), math.log(1.0))), 0.2, 1.0)
    qkv_weight = draw_qkv_weight(jax.random.fold_in(keys[15], 71), 0)
    out_weight = gaussian(keys[9], (HEADS * HEAD, D), (HEADS * HEAD) ** -0.5, 0.125, ((0, 4), (1, 8)))
    gate_up = gaussian(keys[10], (2, D, HID), D ** -0.5, 0.09375, ((1, 8), (2, 4)))
    down_weight = gaussian(keys[11], (HID, D), HID ** -0.5, 0.09375, ((0, 4), (1, 8)))
    merge_gain = jnp.clip(1.0 + 0.1 * jax.random.normal(keys[12], (4, D), jnp.float32), 0.5, 1.5)
    merge_bias = gaussian(keys[13], (4, D), 0.3, 1.5, ((1, 4),), jnp.float32)
    merge_weight = draw_merge_weight(jax.random.fold_in(keys[15], 71), 0)
    return {"tokens": tokens, "grid_sides": grid_sides, "offsets": offsets, "merge_rows": merge_rows, "routes": routes, "norm_gain": norm_gain, "norm_bias": norm_bias, "layer_scale": layer_scale, "qkv_weight": qkv_weight, "out_weight": out_weight, "gate_up": gate_up, "down_weight": down_weight, "merge_gain": merge_gain, "merge_bias": merge_bias, "merge_weight": merge_weight}


EPS = 1e-06

def layer_norm(values, scale_vec, shift_vec):
    center = lax.optimization_barrier(jnp.mean(values, axis=-1, keepdims=True))
    offset_vals = values - center
    spread = lax.optimization_barrier(jnp.mean(offset_vals * offset_vals, axis=-1, keepdims=True))
    return offset_vals * lax.rsqrt(spread + EPS) * scale_vec + shift_vec

def row_layout(grid_part, starts, row_count, head_size):
    position = jnp.arange(row_count, dtype=jnp.int32)
    lengths = 5 + grid_part[:, 0] * grid_part[:, 1]
    inside = ((position[:, None] >= starts[None, :]) & (position[:, None] < (starts + lengths)[None, :])).astype(jnp.int32)
    present = lax.optimization_barrier(jnp.sum(inside, axis=1))
    numbers = jnp.arange(grid_part.shape[0], dtype=jnp.int32)
    image_id = lax.optimization_barrier(jnp.sum(inside * numbers[None, :], axis=1)) + present - 1
    local_row = position - lax.optimization_barrier(jnp.sum(inside * starts[None, :], axis=1))
    height = lax.optimization_barrier(jnp.sum(inside * grid_part[None, :, 0], axis=1)) + 1 - present
    breadth = lax.optimization_barrier(jnp.sum(inside * grid_part[None, :, 1], axis=1)) + 1 - present
    is_patch = (local_row >= 5) & (present > 0)
    patch_idx = jnp.maximum(local_row - 5, 0)
    coord_y = jnp.where(is_patch, (2.0 * (patch_idx // breadth).astype(jnp.float32) + 1.0) / height.astype(jnp.float32) - 1.0, 0.0)
    coord_x = jnp.where(is_patch, (2.0 * (patch_idx % breadth).astype(jnp.float32) + 1.0) / breadth.astype(jnp.float32) - 1.0, 0.0)
    quarter = head_size // 4
    frequency = math.pi * 100.0 ** (-jnp.arange(quarter, dtype=jnp.float32) / quarter)
    angle_y = (coord_y[:, None] * frequency[None, :])[:, None, :]
    angle_x = (coord_x[:, None] * frequency[None, :])[:, None, :]
    return (image_id, (jnp.cos(angle_y), jnp.sin(angle_y), jnp.cos(angle_x), jnp.sin(angle_x)))

def rotate(vectors, tables):
    cos_y, sin_y, cos_x, sin_x = tables
    quarter = vectors.shape[-1] // 4
    upper_y = vectors[..., :quarter]
    lower_y = vectors[..., quarter:2 * quarter]
    upper_x = vectors[..., 2 * quarter:3 * quarter]
    lower_x = vectors[..., 3 * quarter:]
    return jnp.concatenate([upper_y * cos_y - lower_y * sin_y, upper_y * sin_y + lower_y * cos_y, upper_x * cos_x - lower_x * sin_x, upper_x * sin_x + lower_x * cos_x], axis=-1)

def attend(queries, key_rows, values, image_id, numbers):
    scores = jnp.einsum('qhd,khd->hqk', queries.astype(jnp.float32), key_rows.astype(jnp.float32)) / math.sqrt(queries.shape[-1])
    same_image = image_id[:, None] == image_id[None, :]
    scores = jnp.where(same_image[None], scores, -jnp.inf)
    row_peak = lax.optimization_barrier(jnp.max(scores, axis=-1))
    expo_vals = jnp.exp(scores - row_peak[..., None])
    weights = (expo_vals / lax.optimization_barrier(jnp.sum(expo_vals, axis=-1, keepdims=True))).astype(jnp.bfloat16)
    attended = jnp.einsum('hqk,khd->qhd', weights.astype(jnp.float32), values.astype(jnp.float32)).astype(jnp.bfloat16)
    owned = image_id[None, None, :] == numbers[:, None, None]
    logits = lax.optimization_barrier(jnp.max(jnp.where(owned, row_peak[None], -jnp.inf), axis=-1))
    return (attended, logits)

def shard_sum(left_op, right_op):
    parts = jnp.einsum('rsk,skn->srn', left_op.astype(jnp.float32), right_op.astype(jnp.float32))
    rounded = lax.optimization_barrier(parts.astype(jnp.bfloat16))
    return lax.optimization_barrier(jnp.sum(rounded.astype(jnp.float32), axis=0))

def reference(tokens, grid_sides, offsets, merge_rows, routes, norm_gain, norm_bias, layer_scale, qkv_weight, out_weight, gate_up, down_weight, merge_gain, merge_bias, merge_weight):
    shards = N_MLP
    numbers = jnp.arange(IPG, dtype=jnp.int32)
    head_cols = HEADS * HEAD // shards
    feat_cols = D // shards
    out_split = out_weight.reshape(shards, head_cols, D)
    down_split = down_weight.reshape(shards, HID // shards, D)
    merge_split = merge_weight.reshape(4, shards, feat_cols, OUT).transpose(1, 0, 2, 3).reshape(shards, 4 * feat_cols, OUT)

    def one_group(group_id):
        token_block = lax.dynamic_slice_in_dim(tokens, group_id * ROWS, ROWS, 0)
        grid_part = lax.dynamic_slice_in_dim(grid_sides, group_id * IPG, IPG, 0)
        starts = lax.dynamic_slice_in_dim(offsets, group_id * IPG, IPG, 0)
        pick_rows = lax.dynamic_slice_in_dim(merge_rows, group_id * MG, MG, 0)
        image_id, tables = row_layout(grid_part, starts, ROWS, HEAD)
        normed = layer_norm(token_block.astype(jnp.float32), norm_gain[0], norm_bias[0]).astype(jnp.bfloat16)
        mixed_qkv = jnp.dot(normed, qkv_weight, preferred_element_type=jnp.float32).reshape(ROWS, HEADS, 3, HEAD)
        queries = rotate(mixed_qkv[:, :, 0], tables).astype(jnp.bfloat16)
        key_rows = rotate(mixed_qkv[:, :, 1], tables).astype(jnp.bfloat16)
        values = mixed_qkv[:, :, 2].astype(jnp.bfloat16)
        attended, logits = attend(queries, key_rows, values, image_id, numbers)
        attn_sum = shard_sum(attended.reshape(ROWS, shards, head_cols), out_split)
        residual = (token_block.astype(jnp.float32) + layer_scale[0] * attn_sum).astype(jnp.bfloat16)
        normed_two = layer_norm(residual.astype(jnp.float32), norm_gain[1], norm_bias[1]).astype(jnp.bfloat16)
        gate_act = jnp.dot(normed_two, gate_up[0], preferred_element_type=jnp.float32)
        upward = jnp.dot(normed_two, gate_up[1], preferred_element_type=jnp.float32)
        hidden = (jax.nn.silu(gate_act) * upward).astype(jnp.bfloat16)
        ffn_sum = shard_sum(hidden.reshape(ROWS, shards, HID // shards), down_split)
        final_rows = (residual.astype(jnp.float32) + layer_scale[1] * ffn_sum).astype(jnp.bfloat16)
        merged = final_rows[pick_rows].astype(jnp.float32)
        totals = lax.optimization_barrier(jnp.sum(merged, axis=(1, 2)))
        squares = lax.optimization_barrier(jnp.sum(merged * merged, axis=(1, 2)))
        center = totals / (4 * D)
        spread = squares / (4 * D) - center * center
        scaled = ((merged - center[:, None, None]) * lax.rsqrt(spread + EPS)[:, None, None] * merge_gain[None] + merge_bias[None]).astype(jnp.bfloat16)
        scaled_split = scaled.reshape(MG, 4, shards, feat_cols).transpose(0, 2, 1, 3).reshape(MG, shards, 4 * feat_cols)
        projected = shard_sum(scaled_split, merge_split)
        slot_ids = jnp.arange(MG, dtype=jnp.int32)
        owner_grid = grid_part[slot_ids // MSLOT]
        is_live = slot_ids % MSLOT < owner_grid[:, 0] // 2 * (owner_grid[:, 1] // 2)
        projected = jnp.where(is_live[:, None], projected, 0.0).astype(jnp.bfloat16)
        return (projected, logits)
    projected_all, logits_all = lax.map(one_group, jnp.arange(N_REQ, dtype=jnp.int32))
    targets = routes[:, 0].reshape(N_REQ, MG)
    onehot = (targets[:, :, None] == jnp.arange(N_REQ, dtype=jnp.int32)[None, None, :]).astype(jnp.int32)
    before = jnp.cumsum(onehot, axis=1) - onehot
    ranks = lax.optimization_barrier(jnp.sum(before * onehot, axis=2))
    dest_rows = targets * ROUTED + jnp.arange(N_REQ, dtype=jnp.int32)[:, None] * CAP + ranks
    embeds = jnp.zeros((N_REQ * ROUTED, OUT), jnp.bfloat16).at[dest_rows.reshape(-1)].set(projected_all.reshape(N_REQ * MG, OUT))
    token_norms = jnp.sqrt(lax.optimization_barrier(jnp.mean(jnp.square(embeds.astype(jnp.float32)), axis=-1)) + EPS)
    return (embeds, token_norms, logits_all.reshape(IMAGES, HEADS))
```

```python
import functools
import math

import jax
import jax.numpy as jnp
from jax import lax
from jax.experimental import pallas as pl
from jax.experimental.pallas import tpu as pltpu
from jax.sharding import PartitionSpec as P

MESH = pl.DeviceIdType.MESH

HEAD = 128
OUT = 2048
MSLOT = 64
CAP = 16
GMAX = 14


EPS = 1e-06


def layer_norm(values, scale_vec, shift_vec):
    center = jnp.mean(values, axis=-1, keepdims=True)
    offset_vals = values - center
    spread = jnp.mean(offset_vals * offset_vals, axis=-1, keepdims=True)
    return offset_vals * lax.rsqrt(spread + EPS) * scale_vec + shift_vec


def row_layout(grid_part, starts, row_count, head_size):
    position = jnp.arange(row_count, dtype=jnp.int32)
    lengths = 5 + grid_part[:, 0] * grid_part[:, 1]
    inside = (
        (position[:, None] >= starts[None, :]) & (position[:, None] < (starts + lengths)[None, :])
    ).astype(jnp.int32)
    present = jnp.sum(inside, axis=1)
    numbers = jnp.arange(grid_part.shape[0], dtype=jnp.int32)
    image_id = jnp.sum(inside * numbers[None, :], axis=1) + present - 1
    local_row = position - jnp.sum(inside * starts[None, :], axis=1)
    height = jnp.sum(inside * grid_part[None, :, 0], axis=1) + 1 - present
    breadth = jnp.sum(inside * grid_part[None, :, 1], axis=1) + 1 - present
    is_patch = (local_row >= 5) & (present > 0)
    patch_idx = jnp.maximum(local_row - 5, 0)
    coord_y = jnp.where(
        is_patch,
        (2.0 * (patch_idx // breadth).astype(jnp.float32) + 1.0) / height.astype(jnp.float32) - 1.0,
        0.0,
    )
    coord_x = jnp.where(
        is_patch,
        (2.0 * (patch_idx % breadth).astype(jnp.float32) + 1.0) / breadth.astype(jnp.float32) - 1.0,
        0.0,
    )
    quarter = head_size // 4
    frequency = math.pi * 100.0 ** (-jnp.arange(quarter, dtype=jnp.float32) / quarter)
    angle_y = (coord_y[:, None] * frequency[None, :])[:, None, :]
    angle_x = (coord_x[:, None] * frequency[None, :])[:, None, :]
    return (image_id, (jnp.cos(angle_y), jnp.sin(angle_y), jnp.cos(angle_x), jnp.sin(angle_x)))


def rotate(vectors, tables):
    cos_y, sin_y, cos_x, sin_x = tables
    quarter = vectors.shape[-1] // 4
    upper_y = vectors[..., :quarter]
    lower_y = vectors[..., quarter : 2 * quarter]
    upper_x = vectors[..., 2 * quarter : 3 * quarter]
    lower_x = vectors[..., 3 * quarter :]
    return jnp.concatenate(
        [
            upper_y * cos_y - lower_y * sin_y,
            upper_y * sin_y + lower_y * cos_y,
            upper_x * cos_x - lower_x * sin_x,
            upper_x * sin_x + lower_x * cos_x,
        ],
        axis=-1,
    )


def attend(queries, key_rows, values, image_id, numbers):
    scores = jnp.einsum(
        "qhd,khd->hqk", queries, key_rows, preferred_element_type=jnp.float32
    ) / math.sqrt(queries.shape[-1])
    same_image = image_id[:, None] == image_id[None, :]
    scores = jnp.where(same_image[None], scores, -jnp.inf)
    row_peak = jnp.max(scores, axis=-1)
    expo_vals = jnp.exp(scores - row_peak[..., None])
    weights = (expo_vals / jnp.sum(expo_vals, axis=-1, keepdims=True)).astype(jnp.bfloat16)
    attended = jnp.einsum(
        "hqk,khd->qhd", weights, values, preferred_element_type=jnp.float32
    ).astype(jnp.bfloat16)
    owned = image_id[None, None, :] == numbers[:, None, None]
    logits = jnp.max(jnp.where(owned, row_peak[None], -jnp.inf), axis=-1)
    return (attended, logits)


def ring_place(index, n):
    side = index % 2
    return (1 - side) * (index // 2) + side * (n - 1 - index // 2)


def ring_device(place, n):
    wrapped = (place + 2 * n) % n
    late = wrapped // (n // 2)
    return (1 - late) * (2 * wrapped) + late * (2 * (n - 1 - wrapped) + 1)


def region(ref, kind, owner, size, first, count):
    if kind == "col":
        return ref.at[pl.ds(first, count), pl.ds(pl.multiple_of(owner * size, 128), size)]
    rows = pl.ds(pl.multiple_of(owner * size + first, 16), count)
    return ref.at[rows, :] if kind == "row" else ref.at[:, rows, :]


def own_rows(ref, kind, first, count):
    return ref.at[:, pl.ds(first, count), :] if kind == "mid" else ref.at[pl.ds(first, count), :]


def ring_kernel(n, plan, units, extra, *refs):
    count = len(plan)
    ins = refs[:count]
    outs = refs[count + extra : 2 * count + extra]
    send_sem, recv_sem, local_sem = refs[2 * count + extra :]
    me = lax.axis_index("req")
    place = ring_place(me, n)
    right, left = ring_device(place + 1, n), ring_device(place - 1, n)
    barrier = pltpu.get_barrier_semaphore()
    for neighbour in (left, right):
        pl.semaphore_signal(barrier, inc=1, device_id={"req": neighbour}, device_id_type=MESH)
    pl.semaphore_wait(barrier, 2)
    steps = n // 2
    started = {}
    for step in range(steps):
        for u, (i, first, rows) in enumerate(units):
            kind, size = plan[i]
            for way in (0, 1):
                if step > 0:
                    started[u, way, step - 1].wait_recv()
                sign = 1 if way == 0 else -1
                owner = ring_device(place - sign * step, n)
                begin, length = first, rows
                if step == steps - 1:
                    upper = (rows // 2 + 15) // 16 * 16
                    begin, length = (first, upper) if way == 0 else (first + upper, rows - upper)
                target = region(outs[i], kind, owner, size, begin, length)
                copy = pltpu.make_async_remote_copy(
                    src_ref=own_rows(ins[i], kind, begin, length) if step == 0 else target,
                    dst_ref=target,
                    send_sem=send_sem.at[u, way, step],
                    recv_sem=recv_sem.at[u, way, step],
                    device_id={"req": right if way == 0 else left},
                    device_id_type=MESH,
                )
                copy.start()
                started[u, way, step] = copy
        if step == 0:
            local = []
            for i, (kind, size) in enumerate(plan):
                total = ins[i].shape[-2]
                keep = pltpu.make_async_copy(
                    own_rows(ins[i], kind, 0, total),
                    region(outs[i], kind, me, size, 0, total),
                    local_sem.at[i],
                )
                keep.start()
                local.append(keep)
    for (u, way, step), copy in started.items():
        if step == steps - 1:
            copy.wait_recv()
        copy.wait_send()
    for keep in local:
        keep.wait()


def ring_gather(arrays, kinds, cuts, collective_id, after=()):
    n = lax.axis_size("req")
    plan, units, shapes, moved = [], [], [], 0
    for i, (array, kind, cut) in enumerate(zip(arrays, kinds, cuts)):
        axis = array.ndim - 1 if kind == "col" else array.ndim - 2
        shape = list(array.shape)
        plan.append((kind, shape[axis]))
        shape[axis] *= n
        shapes.append(jax.ShapeDtypeStruct(tuple(shape), array.dtype))
        rows = array.shape[-2] // cut
        units += [(i, c * rows, rows) for c in range(cut)]
        moved += math.prod(shape) * 2
    return pl.pallas_call(
        functools.partial(ring_kernel, n, tuple(plan), tuple(units), len(after)),
        out_shape=shapes,
        in_specs=[pl.BlockSpec(memory_space=pl.ANY)] * (len(arrays) + len(after)),
        out_specs=[pl.BlockSpec(memory_space=pl.ANY)] * len(arrays),
        scratch_shapes=[
            pltpu.SemaphoreType.DMA((len(units), 2, n // 2)),
            pltpu.SemaphoreType.DMA((len(units), 2, n // 2)),
            pltpu.SemaphoreType.DMA((len(arrays),)),
        ],
        compiler_params=pltpu.CompilerParams(collective_id=collective_id, has_side_effects=True),
        cost_estimate=pl.CostEstimate(flops=0, bytes_accessed=moved * 12, transcendentals=0),
        name="ring_gather",
    )(*arrays, *after)


def on_device(
    tokens,
    grid_sides,
    offsets,
    merge_rows,
    routes,
    norm_gain,
    norm_bias,
    layer_scale,
    qkv_weight,
    out_weight,
    gate_up,
    down_weight,
    merge_gain,
    merge_bias,
    merge_weight,
):
    images = grid_sides.shape[0]
    row_count = min(tokens.shape[0], -(-images * (5 + GMAX * GMAX) // 16) * 16)
    tokens = tokens[:row_count]
    model_width = tokens.shape[1]
    groups = lax.axis_size("req")
    shards = lax.axis_size("mlp")
    member = lax.axis_index("mlp")
    piece_width = model_width // shards
    start_col = member * piece_width
    slot_count = merge_rows.shape[0]
    numbers = jnp.arange(grid_sides.shape[0], dtype=jnp.int32)
    image_id, tables = row_layout(grid_sides, offsets, row_count, HEAD)
    normed = layer_norm(tokens.astype(jnp.float32), norm_gain[0], norm_bias[0]).astype(jnp.bfloat16)
    columns = normed
    qkv_all, out_all = ring_gather([qkv_weight, out_weight], ["row", "col"], [2, 1], 0)
    mixed_qkv = jnp.dot(
        columns,
        qkv_all,
        preferred_element_type=jnp.float32,
    )
    heads_here = qkv_weight.shape[1] // (3 * HEAD)
    mixed_qkv = mixed_qkv.reshape(row_count, heads_here, 3, HEAD)
    queries = rotate(mixed_qkv[:, :, 0], tables).astype(jnp.bfloat16)
    key_rows = rotate(mixed_qkv[:, :, 1], tables).astype(jnp.bfloat16)
    values = mixed_qkv[:, :, 2].astype(jnp.bfloat16)
    attended, logits = attend(queries, key_rows, values, image_id, numbers)
    attended_flat = attended.reshape(row_count, heads_here * HEAD)
    head_terms = jnp.dot(
        attended_flat,
        out_all,
        preferred_element_type=jnp.float32,
    ).astype(jnp.bfloat16)
    gate_all, down_all = ring_gather(
        [gate_up, down_weight], ["mid", "col"], [2, 2], 1, after=(head_terms[:16, :128],)
    )
    attn_sum = lax.psum(head_terms, "mlp").astype(jnp.float32)
    residual = (tokens.astype(jnp.float32) + layer_scale[0] * attn_sum).astype(jnp.bfloat16)
    resid_piece = lax.dynamic_slice_in_dim(residual, start_col, piece_width, 1)
    normed_two = layer_norm(residual.astype(jnp.float32), norm_gain[1], norm_bias[1]).astype(
        jnp.bfloat16
    )
    columns = normed_two
    gate_pair = jnp.einsum(
        "rk,pkn->prn",
        columns,
        gate_all,
        preferred_element_type=jnp.float32,
    )
    hidden = (jax.nn.silu(gate_pair[0]) * gate_pair[1]).astype(jnp.bfloat16)
    hidden_terms = jnp.dot(
        hidden,
        down_all,
        preferred_element_type=jnp.float32,
    )
    ffn_piece = lax.psum_scatter(
        hidden_terms.astype(jnp.bfloat16), "mlp", scatter_dimension=1, tiled=True
    ).astype(jnp.float32)
    own_scale_two = lax.dynamic_slice_in_dim(layer_scale[1], start_col, piece_width, 0)
    final_piece = (resid_piece.astype(jnp.float32) + own_scale_two * ffn_piece).astype(jnp.bfloat16)
    live = -(-(GMAX // 2) ** 2 // 8) * 8
    picked = merge_rows.reshape(images, MSLOT, 4)[:, :live].reshape(images * live, 4)
    merged = final_piece[picked].astype(jnp.float32)
    totals, squares = lax.psum(
        (jnp.sum(merged, axis=(1, 2)), jnp.sum(merged * merged, axis=(1, 2))), "mlp"
    )
    center = totals / (4 * model_width)
    spread = squares / (4 * model_width) - center * center
    scaled = (
        (merged - center[:, None, None]) * lax.rsqrt(spread + EPS)[:, None, None] * merge_gain[None]
        + merge_bias[None]
    )
    sent = images * live
    is_live = (
        jnp.arange(live, dtype=jnp.int32)[None, :]
        < (grid_sides[:, 0] // 2 * (grid_sides[:, 1] // 2))[:, None]
    ).reshape(sent)
    scaled = jnp.where(is_live[:, None, None], scaled, 0.0).astype(jnp.bfloat16)
    (scaled_all,) = ring_gather([scaled.reshape(sent, 4 * piece_width)], ["row"], [1], 2)
    merge_terms = jnp.dot(
        scaled_all,
        merge_weight.reshape(4 * piece_width, merge_weight.shape[2]),
        preferred_element_type=jnp.float32,
    ).astype(jnp.bfloat16)
    targets = routes[:, 0].reshape(groups, slot_count)
    earlier = jnp.arange(slot_count)[None, :] < jnp.arange(slot_count)[:, None]
    same = (targets[:, :, None] == targets[:, None, :]) & earlier[None]
    ranks = jnp.sum(same.astype(jnp.int32), axis=2)
    rows_out = groups * CAP
    dest = targets * rows_out + jnp.arange(groups, dtype=jnp.int32)[:, None] * CAP + ranks
    dest = dest.reshape(groups, images, MSLOT)[:, :, :live].reshape(groups * sent)
    chosen = (jnp.arange(groups * rows_out, dtype=jnp.int32)[:, None] == dest[None, :]).astype(
        jnp.bfloat16
    )
    placed_rows = jnp.dot(chosen, merge_terms, preferred_element_type=jnp.float32).astype(
        jnp.bfloat16
    )
    received = lax.all_to_all(
        placed_rows.reshape(groups, rows_out, merge_terms.shape[1]),
        "req",
        split_axis=0,
        concat_axis=0,
        tiled=True,
    )
    partial = received.transpose(1, 0, 2).reshape(rows_out, groups * merge_terms.shape[1])
    embeds = lax.psum_scatter(partial, "mlp", scatter_dimension=1, tiled=True)
    row_squares = jnp.sum(jnp.square(embeds.astype(jnp.float32)), axis=1)
    total_squares = lax.psum(row_squares, "mlp")
    token_norms = jnp.sqrt(total_squares / OUT + EPS)
    return (embeds, token_norms, logits)


def solution(mesh):
    placed = (
        P("req", None),
        P("req", None),
        P("req"),
        P("req", None),
        P(),
        P(),
        P(),
        P(),
        P("req", "mlp"),
        P("mlp", "req"),
        P(None, "req", "mlp"),
        P("mlp", "req"),
        P(None, "mlp"),
        P(None, "mlp"),
        P(None, "mlp", "req"),
    )
    return jax.shard_map(
        on_device,
        mesh=mesh,
        in_specs=placed,
        out_specs=(P("req", "mlp"), P("req"), P("req", "mlp")),
        check_vma=False,
    )
```

```python
import functools
import math

import jax
import jax.numpy as jnp
from jax import lax
from jax.experimental import pallas as pl
from jax.experimental.pallas import tpu as pltpu
from jax.sharding import PartitionSpec as P

MESH = pl.DeviceIdType.MESH

HEAD = 128
OUT = 2048
MSLOT = 64
CAP = 16
GMAX = 14


EPS = 1e-06


def layer_norm(values, scale_vec, shift_vec):
    center = jnp.mean(values, axis=-1, keepdims=True)
    offset_vals = values - center
    spread = jnp.mean(offset_vals * offset_vals, axis=-1, keepdims=True)
    return offset_vals * lax.rsqrt(spread + EPS) * scale_vec + shift_vec


def row_layout(grid_part, starts, row_count, head_size):
    position = jnp.arange(row_count, dtype=jnp.int32)
    lengths = 5 + grid_part[:, 0] * grid_part[:, 1]
    inside = (
        (position[:, None] >= starts[None, :]) & (position[:, None] < (starts + lengths)[None, :])
    ).astype(jnp.int32)
    present = jnp.sum(inside, axis=1)
    numbers = jnp.arange(grid_part.shape[0], dtype=jnp.int32)
    image_id = jnp.sum(inside * numbers[None, :], axis=1) + present - 1
    local_row = position - jnp.sum(inside * starts[None, :], axis=1)
    height = jnp.sum(inside * grid_part[None, :, 0], axis=1) + 1 - present
    breadth = jnp.sum(inside * grid_part[None, :, 1], axis=1) + 1 - present
    is_patch = (local_row >= 5) & (present > 0)
    patch_idx = jnp.maximum(local_row - 5, 0)
    coord_y = jnp.where(
        is_patch,
        (2.0 * (patch_idx // breadth).astype(jnp.float32) + 1.0) / height.astype(jnp.float32) - 1.0,
        0.0,
    )
    coord_x = jnp.where(
        is_patch,
        (2.0 * (patch_idx % breadth).astype(jnp.float32) + 1.0) / breadth.astype(jnp.float32) - 1.0,
        0.0,
    )
    quarter = head_size // 4
    frequency = math.pi * 100.0 ** (-jnp.arange(quarter, dtype=jnp.float32) / quarter)
    angle_y = (coord_y[:, None] * frequency[None, :])[:, None, :]
    angle_x = (coord_x[:, None] * frequency[None, :])[:, None, :]
    return (image_id, (jnp.cos(angle_y), jnp.sin(angle_y), jnp.cos(angle_x), jnp.sin(angle_x)))


def rotate(vectors, tables):
    cos_y, sin_y, cos_x, sin_x = tables
    quarter = vectors.shape[-1] // 4
    upper_y = vectors[..., :quarter]
    lower_y = vectors[..., quarter : 2 * quarter]
    upper_x = vectors[..., 2 * quarter : 3 * quarter]
    lower_x = vectors[..., 3 * quarter :]
    return jnp.concatenate(
        [
            upper_y * cos_y - lower_y * sin_y,
            upper_y * sin_y + lower_y * cos_y,
            upper_x * cos_x - lower_x * sin_x,
            upper_x * sin_x + lower_x * cos_x,
        ],
        axis=-1,
    )


def attend(queries, key_rows, values, image_id, numbers):
    scores = jnp.einsum(
        "qhd,khd->hqk", queries, key_rows, preferred_element_type=jnp.float32
    ) / math.sqrt(queries.shape[-1])
    same_image = image_id[:, None] == image_id[None, :]
    scores = jnp.where(same_image[None], scores, -jnp.inf)
    row_peak = jnp.max(scores, axis=-1)
    expo_vals = jnp.exp(scores - row_peak[..., None])
    weights = (expo_vals / jnp.sum(expo_vals, axis=-1, keepdims=True)).astype(jnp.bfloat16)
    attended = jnp.einsum(
        "hqk,khd->qhd", weights, values, preferred_element_type=jnp.float32
    ).astype(jnp.bfloat16)
    owned = image_id[None, None, :] == numbers[:, None, None]
    logits = jnp.max(jnp.where(owned, row_peak[None], -jnp.inf), axis=-1)
    return (attended, logits)


def ring_place(index, n):
    side = index % 2
    return (1 - side) * (index // 2) + side * (n - 1 - index // 2)


def ring_device(place, n):
    wrapped = (place + 2 * n) % n
    late = wrapped // (n // 2)
    return (1 - late) * (2 * wrapped) + late * (2 * (n - 1 - wrapped) + 1)


def region(ref, kind, owner, size, first, count):
    if kind == "col":
        return ref.at[pl.ds(first, count), pl.ds(pl.multiple_of(owner * size, 128), size)]
    rows = pl.ds(pl.multiple_of(owner * size + first, 16), count)
    return ref.at[rows, :] if kind == "row" else ref.at[:, rows, :]


def own_rows(ref, kind, first, count):
    return ref.at[:, pl.ds(first, count), :] if kind == "mid" else ref.at[pl.ds(first, count), :]


def ring_steps(n, plan, units, ins, outs, send_sem, recv_sem, local_sem, work=None):
    me = lax.axis_index("req")
    place = ring_place(me, n)
    right, left = ring_device(place + 1, n), ring_device(place - 1, n)
    barrier = pltpu.get_barrier_semaphore()
    for neighbour in (left, right):
        pl.semaphore_signal(barrier, inc=1, device_id={"req": neighbour}, device_id_type=MESH)
    pl.semaphore_wait(barrier, 2)
    steps = n // 2
    started = {}
    for step in range(steps):
        for u, (i, first, rows) in enumerate(units):
            kind, size = plan[i]
            for way in (0, 1):
                if step > 0:
                    started[u, way, step - 1].wait_recv()
                sign = 1 if way == 0 else -1
                owner = ring_device(place - sign * step, n)
                begin, length = first, rows
                if step == steps - 1:
                    upper = (rows // 2 + 15) // 16 * 16
                    begin, length = (first, upper) if way == 0 else (first + upper, rows - upper)
                target = region(outs[i], kind, owner, size, begin, length)
                copy = pltpu.make_async_remote_copy(
                    src_ref=own_rows(ins[i], kind, begin, length) if step == 0 else target,
                    dst_ref=target,
                    send_sem=send_sem.at[u, way, step],
                    recv_sem=recv_sem.at[u, way, step],
                    device_id={"req": right if way == 0 else left},
                    device_id_type=MESH,
                )
                copy.start()
                started[u, way, step] = copy
        if step == 0:
            local = []
            for i, (kind, size) in enumerate(plan):
                total = ins[i].shape[-2]
                keep = pltpu.make_async_copy(
                    own_rows(ins[i], kind, 0, total),
                    region(outs[i], kind, me, size, 0, total),
                    local_sem.at[i],
                )
                keep.start()
                local.append(keep)
        if work is not None:
            if step == 0:
                local.pop(0).wait()
                work(step, me, me)
            else:
                work(step, ring_device(place - step, n), ring_device(place + step, n))
    for (u, way, step), copy in started.items():
        if step == steps - 1:
            copy.wait_recv()
        copy.wait_send()
    for keep in local:
        keep.wait()
    if work is not None:
        last = ring_device(place + steps, n)
        work(steps, last, last)


def ring_kernel(n, plan, units, extra, *refs):
    count = len(plan)
    ring_steps(
        n,
        plan,
        units,
        refs[:count],
        refs[count + extra : 2 * count + extra],
        *refs[2 * count + extra :],
    )


def project_kernel(
    n,
    plan,
    units,
    tokens_ref,
    gain_ref,
    bias_ref,
    weight_ref,
    out_weight_ref,
    mixed_ref,
    out_all_ref,
    normed,
    gathered,
    send_sem,
    recv_sem,
    local_sem,
):
    depth, width = weight_ref.shape
    tile = 256

    def norm_rows(block, carry):
        rows = pl.ds(pl.multiple_of(block * 16, 16), 16)
        normed[rows, :] = layer_norm(
            tokens_ref[rows, :].astype(jnp.float32), gain_ref[...], bias_ref[...]
        ).astype(jnp.bfloat16)
        return carry

    def multiply(owner, first):
        part = pl.ds(pl.multiple_of(owner * depth, 128), depth)

        def column_tile(index, carry):
            columns = pl.ds(pl.multiple_of(index * tile, 128), tile)
            product = jnp.dot(
                normed[:, part], gathered[part, columns], preferred_element_type=jnp.float32
            )
            mixed_ref[:, columns] = product if first else mixed_ref[:, columns] + product
            return carry

        lax.fori_loop(0, width // tile, column_tile, 0)

    def work(step, one, other):
        if step == 0:
            lax.fori_loop(0, tokens_ref.shape[0] // 16, norm_rows, 0)
        multiply(one, step == 0)
        if 0 < step < n // 2:
            multiply(other, False)

    ring_steps(
        n,
        plan,
        units,
        (weight_ref, out_weight_ref),
        (gathered, out_all_ref),
        send_sem,
        recv_sem,
        local_sem,
        work,
    )


def norm_project(tokens, gain, bias, qkv_weight, out_weight):
    n = lax.axis_size("req")
    rows, model_width = tokens.shape
    depth, width = qkv_weight.shape
    plan = (("row", depth), ("col", out_weight.shape[1]))
    units = ((0, 0, depth // 2), (0, depth // 2, depth // 2), (1, 0, out_weight.shape[0]))
    anywhere, vmem = pl.BlockSpec(memory_space=pl.ANY), pl.BlockSpec(memory_space=pltpu.VMEM)
    return pl.pallas_call(
        functools.partial(project_kernel, n, plan, units),
        out_shape=(
            jax.ShapeDtypeStruct((rows, width), jnp.float32),
            jax.ShapeDtypeStruct((out_weight.shape[0], n * out_weight.shape[1]), jnp.bfloat16),
        ),
        in_specs=[vmem, vmem, vmem, anywhere, anywhere],
        out_specs=(vmem, anywhere),
        scratch_shapes=[
            pltpu.VMEM((rows, model_width), jnp.bfloat16),
            pltpu.VMEM((n * depth, width), jnp.bfloat16),
            pltpu.SemaphoreType.DMA((len(units), 2, n // 2)),
            pltpu.SemaphoreType.DMA((len(units), 2, n // 2)),
            pltpu.SemaphoreType.DMA((2,)),
        ],
        compiler_params=pltpu.CompilerParams(
            collective_id=0, has_side_effects=True, vmem_limit_bytes=48 * 2**20
        ),
        cost_estimate=pl.CostEstimate(
            flops=2 * rows * model_width * width, bytes_accessed=300 * 2**20, transcendentals=0
        ),
        name="norm_project",
    )(tokens, gain, bias, qkv_weight, out_weight)


def ring_gather(arrays, kinds, cuts, collective_id, after=()):
    n = lax.axis_size("req")
    plan, units, shapes, moved = [], [], [], 0
    for i, (array, kind, cut) in enumerate(zip(arrays, kinds, cuts)):
        axis = array.ndim - 1 if kind == "col" else array.ndim - 2
        shape = list(array.shape)
        plan.append((kind, shape[axis]))
        shape[axis] *= n
        shapes.append(jax.ShapeDtypeStruct(tuple(shape), array.dtype))
        rows = array.shape[-2] // cut
        units += [(i, c * rows, rows) for c in range(cut)]
        moved += math.prod(shape) * 2
    return pl.pallas_call(
        functools.partial(ring_kernel, n, tuple(plan), tuple(units), len(after)),
        out_shape=shapes,
        in_specs=[pl.BlockSpec(memory_space=pl.ANY)] * (len(arrays) + len(after)),
        out_specs=[pl.BlockSpec(memory_space=pl.ANY)] * len(arrays),
        scratch_shapes=[
            pltpu.SemaphoreType.DMA((len(units), 2, n // 2)),
            pltpu.SemaphoreType.DMA((len(units), 2, n // 2)),
            pltpu.SemaphoreType.DMA((len(arrays),)),
        ],
        compiler_params=pltpu.CompilerParams(collective_id=collective_id, has_side_effects=True),
        cost_estimate=pl.CostEstimate(flops=0, bytes_accessed=moved * 12, transcendentals=0),
        name="ring_gather",
    )(*arrays, *after)


def on_device(
    tokens,
    grid_sides,
    offsets,
    merge_rows,
    routes,
    norm_gain,
    norm_bias,
    layer_scale,
    qkv_weight,
    out_weight,
    gate_up,
    down_weight,
    merge_gain,
    merge_bias,
    merge_weight,
):
    images = grid_sides.shape[0]
    row_count = min(tokens.shape[0], -(-images * (5 + GMAX * GMAX) // 16) * 16)
    tokens = tokens[:row_count]
    model_width = tokens.shape[1]
    groups = lax.axis_size("req")
    shards = lax.axis_size("mlp")
    member = lax.axis_index("mlp")
    piece_width = model_width // shards
    start_col = member * piece_width
    slot_count = merge_rows.shape[0]
    numbers = jnp.arange(grid_sides.shape[0], dtype=jnp.int32)
    image_id, tables = row_layout(grid_sides, offsets, row_count, HEAD)
    mixed_qkv, out_all = norm_project(
        tokens, norm_gain[:1], norm_bias[:1], qkv_weight, out_weight
    )
    heads_here = qkv_weight.shape[1] // (3 * HEAD)
    mixed_qkv = mixed_qkv.reshape(row_count, heads_here, 3, HEAD)
    queries = rotate(mixed_qkv[:, :, 0], tables).astype(jnp.bfloat16)
    key_rows = rotate(mixed_qkv[:, :, 1], tables).astype(jnp.bfloat16)
    values = mixed_qkv[:, :, 2].astype(jnp.bfloat16)
    attended, logits = attend(queries, key_rows, values, image_id, numbers)
    attended_flat = attended.reshape(row_count, heads_here * HEAD)
    head_terms = jnp.dot(
        attended_flat,
        out_all,
        preferred_element_type=jnp.float32,
    ).astype(jnp.bfloat16)
    gate_all, down_all = ring_gather(
        [gate_up, down_weight], ["mid", "col"], [2, 2], 1, after=(head_terms[:16, :128],)
    )
    attn_sum = lax.psum(head_terms, "mlp").astype(jnp.float32)
    residual = (tokens.astype(jnp.float32) + layer_scale[0] * attn_sum).astype(jnp.bfloat16)
    resid_piece = lax.dynamic_slice_in_dim(residual, start_col, piece_width, 1)
    normed_two = layer_norm(residual.astype(jnp.float32), norm_gain[1], norm_bias[1]).astype(
        jnp.bfloat16
    )
    columns = normed_two
    gate_pair = jnp.einsum(
        "rk,pkn->prn",
        columns,
        gate_all,
        preferred_element_type=jnp.float32,
    )
    hidden = (jax.nn.silu(gate_pair[0]) * gate_pair[1]).astype(jnp.bfloat16)
    hidden_terms = jnp.dot(hidden, down_all, preferred_element_type=jnp.float32)
    ffn_piece = lax.psum_scatter(
        hidden_terms.astype(jnp.bfloat16), "mlp", scatter_dimension=1, tiled=True
    ).astype(jnp.float32)
    own_scale_two = lax.dynamic_slice_in_dim(layer_scale[1], start_col, piece_width, 0)
    final_piece = (resid_piece.astype(jnp.float32) + own_scale_two * ffn_piece).astype(jnp.bfloat16)
    live = -(-(GMAX // 2) ** 2 // 8) * 8
    picked = merge_rows.reshape(images, MSLOT, 4)[:, :live].reshape(images * live, 4)
    merged = final_piece[picked].astype(jnp.float32)
    totals, squares = lax.psum(
        (jnp.sum(merged, axis=(1, 2)), jnp.sum(merged * merged, axis=(1, 2))), "mlp"
    )
    center = totals / (4 * model_width)
    spread = squares / (4 * model_width) - center * center
    scaled = (
        (merged - center[:, None, None]) * lax.rsqrt(spread + EPS)[:, None, None] * merge_gain[None]
        + merge_bias[None]
    )
    sent = images * live
    is_live = (
        jnp.arange(live, dtype=jnp.int32)[None, :]
        < (grid_sides[:, 0] // 2 * (grid_sides[:, 1] // 2))[:, None]
    ).reshape(sent)
    scaled = jnp.where(is_live[:, None, None], scaled, 0.0).astype(jnp.bfloat16)
    (scaled_all,) = ring_gather([scaled.reshape(sent, 4 * piece_width)], ["row"], [1], 2)
    merge_terms = jnp.dot(
        scaled_all,
        merge_weight.reshape(4 * piece_width, merge_weight.shape[2]),
        preferred_element_type=jnp.float32,
    ).astype(jnp.bfloat16)
    targets = routes[:, 0].reshape(groups, slot_count)
    earlier = jnp.arange(slot_count)[None, :] < jnp.arange(slot_count)[:, None]
    same = (targets[:, :, None] == targets[:, None, :]) & earlier[None]
    ranks = jnp.sum(same.astype(jnp.int32), axis=2)
    rows_out = groups * CAP
    dest = targets * rows_out + jnp.arange(groups, dtype=jnp.int32)[:, None] * CAP + ranks
    dest = dest.reshape(groups, images, MSLOT)[:, :, :live].reshape(groups * sent)
    chosen = (jnp.arange(groups * rows_out, dtype=jnp.int32)[:, None] == dest[None, :]).astype(
        jnp.bfloat16
    )
    placed_rows = jnp.dot(chosen, merge_terms, preferred_element_type=jnp.float32).astype(
        jnp.bfloat16
    )
    received = lax.all_to_all(
        placed_rows.reshape(groups, rows_out, merge_terms.shape[1]),
        "req",
        split_axis=0,
        concat_axis=0,
        tiled=True,
    )
    terms = lax.all_to_all(received, "mlp", split_axis=0, concat_axis=0, tiled=True)
    terms = terms.reshape(shards, groups // shards, rows_out, merge_terms.shape[1])
    embeds = jnp.sum(terms.astype(jnp.float32), axis=0).astype(jnp.bfloat16)
    embeds = embeds.transpose(1, 0, 2).reshape(rows_out, OUT // shards)
    row_squares = jnp.sum(jnp.square(embeds.astype(jnp.float32)), axis=1)
    total_squares = lax.psum(row_squares, "mlp")
    token_norms = jnp.sqrt(total_squares / OUT + EPS)
    return (embeds, token_norms, logits)


def solution(mesh):
    placed = (
        P("req", None),
        P("req", None),
        P("req"),
        P("req", None),
        P(),
        P(),
        P(),
        P(),
        P("req", "mlp"),
        P("mlp", "req"),
        P(None, "req", "mlp"),
        P("mlp", "req"),
        P(None, "mlp"),
        P(None, "mlp"),
        P(None, "mlp", "req"),
    )
    return jax.shard_map(
        on_device,
        mesh=mesh,
        in_specs=placed,
        out_specs=(P("req", "mlp"), P("req"), P("req", "mlp")),
        check_vma=False,
    )
```

```python
import functools
import math

import jax
import jax.numpy as jnp
from jax import lax
from jax.experimental import pallas as pl
from jax.experimental.pallas import tpu as pltpu
from jax.sharding import PartitionSpec as P

MESH = pl.DeviceIdType.MESH

HEAD = 128
OUT = 2048
MSLOT = 64
CAP = 16
GMAX = 14


EPS = 1e-06


def layer_norm(values, scale_vec, shift_vec):
    center = jnp.mean(values, axis=-1, keepdims=True)
    offset_vals = values - center
    spread = jnp.mean(offset_vals * offset_vals, axis=-1, keepdims=True)
    return offset_vals * lax.rsqrt(spread + EPS) * scale_vec + shift_vec


def row_layout(grid_part, starts, row_count, head_size):
    position = jnp.arange(row_count, dtype=jnp.int32)
    lengths = 5 + grid_part[:, 0] * grid_part[:, 1]
    inside = (
        (position[:, None] >= starts[None, :]) & (position[:, None] < (starts + lengths)[None, :])
    ).astype(jnp.int32)
    present = jnp.sum(inside, axis=1)
    numbers = jnp.arange(grid_part.shape[0], dtype=jnp.int32)
    image_id = jnp.sum(inside * numbers[None, :], axis=1) + present - 1
    local_row = position - jnp.sum(inside * starts[None, :], axis=1)
    height = jnp.sum(inside * grid_part[None, :, 0], axis=1) + 1 - present
    breadth = jnp.sum(inside * grid_part[None, :, 1], axis=1) + 1 - present
    is_patch = (local_row >= 5) & (present > 0)
    patch_idx = jnp.maximum(local_row - 5, 0)
    coord_y = jnp.where(
        is_patch,
        (2.0 * (patch_idx // breadth).astype(jnp.float32) + 1.0) / height.astype(jnp.float32) - 1.0,
        0.0,
    )
    coord_x = jnp.where(
        is_patch,
        (2.0 * (patch_idx % breadth).astype(jnp.float32) + 1.0) / breadth.astype(jnp.float32) - 1.0,
        0.0,
    )
    quarter = head_size // 4
    frequency = math.pi * 100.0 ** (-jnp.arange(quarter, dtype=jnp.float32) / quarter)
    angle_y = (coord_y[:, None] * frequency[None, :])[:, None, :]
    angle_x = (coord_x[:, None] * frequency[None, :])[:, None, :]
    return (image_id, (jnp.cos(angle_y), jnp.sin(angle_y), jnp.cos(angle_x), jnp.sin(angle_x)))


def attend(queries, key_rows, values, image_id, numbers):
    scores = jnp.einsum(
        "hqd,hkd->hqk", queries, key_rows, preferred_element_type=jnp.float32
    ) / math.sqrt(queries.shape[-1])
    same_image = image_id[:, None] == image_id[None, :]
    scores = jnp.where(same_image[None], scores, -jnp.inf)
    row_peak = jnp.max(scores, axis=-1)
    expo_vals = jnp.exp(scores - row_peak[..., None])
    weights = (expo_vals / jnp.sum(expo_vals, axis=-1, keepdims=True)).astype(jnp.bfloat16)
    attended = jnp.einsum(
        "hqk,hkd->qhd", weights, values, preferred_element_type=jnp.float32
    ).astype(jnp.bfloat16)
    owned = image_id[None, None, :] == numbers[:, None, None]
    logits = jnp.max(jnp.where(owned, row_peak[None], -jnp.inf), axis=-1)
    return (attended, logits)


def ring_place(index, n):
    side = index % 2
    return (1 - side) * (index // 2) + side * (n - 1 - index // 2)


def ring_device(place, n):
    wrapped = (place + 2 * n) % n
    late = wrapped // (n // 2)
    return (1 - late) * (2 * wrapped) + late * (2 * (n - 1 - wrapped) + 1)


def region(ref, kind, owner, size, first, count):
    if kind == "col":
        return ref.at[pl.ds(first, count), pl.ds(pl.multiple_of(owner * size, 128), size)]
    rows = pl.ds(pl.multiple_of(owner * size + first, 16), count)
    return ref.at[rows, :] if kind == "row" else ref.at[:, rows, :]


def own_rows(ref, kind, first, count):
    return ref.at[:, pl.ds(first, count), :] if kind == "mid" else ref.at[pl.ds(first, count), :]


def ring_steps(n, plan, units, ins, outs, send_sem, recv_sem, local_sem, work=None):
    me = lax.axis_index("req")
    place = ring_place(me, n)
    right, left = ring_device(place + 1, n), ring_device(place - 1, n)
    barrier = pltpu.get_barrier_semaphore()
    for neighbour in (left, right):
        pl.semaphore_signal(barrier, inc=1, device_id={"req": neighbour}, device_id_type=MESH)
    pl.semaphore_wait(barrier, 2)
    steps = n // 2
    started = {}
    for step in range(steps):
        for u, (i, first, rows) in enumerate(units):
            kind, size = plan[i]
            for way in (0, 1):
                if step > 0:
                    started[u, way, step - 1].wait_recv()
                sign = 1 if way == 0 else -1
                owner = ring_device(place - sign * step, n)
                begin, length = first, rows
                if step == steps - 1:
                    upper = (rows // 2 + 15) // 16 * 16
                    begin, length = (first, upper) if way == 0 else (first + upper, rows - upper)
                target = region(outs[i], kind, owner, size, begin, length)
                copy = pltpu.make_async_remote_copy(
                    src_ref=own_rows(ins[i], kind, begin, length) if step == 0 else target,
                    dst_ref=target,
                    send_sem=send_sem.at[u, way, step],
                    recv_sem=recv_sem.at[u, way, step],
                    device_id={"req": right if way == 0 else left},
                    device_id_type=MESH,
                )
                copy.start()
                started[u, way, step] = copy
        if step == 0:
            local = []
            for i, (kind, size) in enumerate(plan):
                total = ins[i].shape[-2]
                keep = pltpu.make_async_copy(
                    own_rows(ins[i], kind, 0, total),
                    region(outs[i], kind, me, size, 0, total),
                    local_sem.at[i],
                )
                keep.start()
                local.append(keep)
        if work is not None:
            if step == 0:
                local.pop(0).wait()
                work(step, me, me)
            else:
                work(step, ring_device(place - step, n), ring_device(place + step, n))
    for (u, way, step), copy in started.items():
        if step == steps - 1:
            copy.wait_recv()
        copy.wait_send()
    for keep in local:
        keep.wait()
    if work is not None:
        last = ring_device(place + steps, n)
        work(steps, last, last)


def ring_kernel(n, plan, units, extra, *refs):
    count = len(plan)
    ring_steps(
        n,
        plan,
        units,
        refs[:count],
        refs[count + extra : 2 * count + extra],
        *refs[2 * count + extra :],
    )


def project_kernel(
    n,
    plan,
    units,
    tokens_ref,
    gain_ref,
    bias_ref,
    weight_ref,
    out_weight_ref,
    cos_ref,
    sin_ref,
    queries_ref,
    keys_ref,
    values_ref,
    out_all_ref,
    tokens_in,
    mixed_ref,
    normed,
    gathered,
    send_sem,
    recv_sem,
    local_sem,
    tokens_sem,
):
    depth, width = weight_ref.shape
    tile = 256

    def norm_rows(block, carry):
        rows = pl.ds(pl.multiple_of(block * 16, 16), 16)
        normed[rows, :] = layer_norm(
            tokens_in[rows, :].astype(jnp.float32), gain_ref[...], bias_ref[...]
        ).astype(jnp.bfloat16)
        return carry

    def multiply(owner, first):
        part = pl.ds(pl.multiple_of(owner * depth, 128), depth)

        def column_tile(index, carry):
            columns = pl.ds(pl.multiple_of(index * tile, 128), tile)
            product = jnp.dot(
                normed[:, part], gathered[part, columns], preferred_element_type=jnp.float32
            )
            mixed_ref[:, columns] = product if first else mixed_ref[:, columns] + product
            return carry

        lax.fori_loop(0, width // tile, column_tile, 0)

    def work(step, one, other):
        if step == 0:
            fetch.wait()
            lax.fori_loop(0, tokens_in.shape[0] // 16, norm_rows, 0)
        multiply(one, step == 0)
        if 0 < step < n // 2:
            multiply(other, False)

    fetch = pltpu.make_async_copy(
        tokens_ref.at[pl.ds(0, tokens_in.shape[0]), :], tokens_in, tokens_sem.at[0]
    )
    fetch.start()
    ring_steps(
        n,
        plan,
        units,
        (weight_ref, out_weight_ref),
        (gathered, out_all_ref),
        send_sem,
        recv_sem,
        local_sem,
        work,
    )
    lane = lax.broadcasted_iota(jnp.int32, (1, HEAD), 1)
    leading = lane // (HEAD // 4) % 2 == 0
    for head in range(width // (3 * HEAD)):
        for j, target in enumerate((queries_ref, keys_ref)):
            vectors = mixed_ref[:, (3 * head + j) * HEAD : (3 * head + j + 1) * HEAD]
            partner = jnp.where(
                leading,
                pltpu.roll(vectors, HEAD - HEAD // 4, 1),
                pltpu.roll(vectors, HEAD // 4, 1),
            )
            target[head] = (vectors * cos_ref[...] + partner * sin_ref[...]).astype(jnp.bfloat16)
        values_ref[head] = mixed_ref[:, (3 * head + 2) * HEAD : (3 * head + 3) * HEAD].astype(
            jnp.bfloat16
        )


def norm_project(tokens, rows, gain, bias, qkv_weight, out_weight, cosines, sines):
    n = lax.axis_size("req")
    model_width = tokens.shape[1]
    depth, width = qkv_weight.shape
    plan = (("row", depth), ("col", out_weight.shape[1]))
    units = ((0, 0, depth // 2), (0, depth // 2, depth // 2), (1, 0, out_weight.shape[0]))
    heads = width // (3 * HEAD)
    by_head = jax.ShapeDtypeStruct((heads, rows, HEAD), jnp.bfloat16)
    anywhere, vmem = pl.BlockSpec(memory_space=pl.ANY), pl.BlockSpec(memory_space=pltpu.VMEM)
    return pl.pallas_call(
        functools.partial(project_kernel, n, plan, units),
        out_shape=(
            by_head,
            by_head,
            by_head,
            jax.ShapeDtypeStruct((out_weight.shape[0], n * out_weight.shape[1]), jnp.bfloat16),
        ),
        in_specs=[anywhere, vmem, vmem, anywhere, anywhere, vmem, vmem],
        out_specs=(vmem, vmem, vmem, anywhere),
        scratch_shapes=[
            pltpu.VMEM((rows, model_width), jnp.bfloat16),
            pltpu.VMEM((rows, width), jnp.float32),
            pltpu.VMEM((rows, model_width), jnp.bfloat16),
            pltpu.VMEM((n * depth, width), jnp.bfloat16),
            pltpu.SemaphoreType.DMA((len(units), 2, n // 2)),
            pltpu.SemaphoreType.DMA((len(units), 2, n // 2)),
            pltpu.SemaphoreType.DMA((2,)),
            pltpu.SemaphoreType.DMA((1,)),
        ],
        compiler_params=pltpu.CompilerParams(
            collective_id=0, has_side_effects=True, vmem_limit_bytes=48 * 2**20
        ),
        cost_estimate=pl.CostEstimate(
            flops=2 * rows * model_width * width, bytes_accessed=300 * 2**20, transcendentals=0
        ),
        name="norm_project",
    )(tokens, gain, bias, qkv_weight, out_weight, cosines, sines)


def ring_gather(arrays, kinds, cuts, collective_id, after=()):
    n = lax.axis_size("req")
    plan, units, shapes, moved = [], [], [], 0
    for i, (array, kind, cut) in enumerate(zip(arrays, kinds, cuts)):
        axis = array.ndim - 1 if kind == "col" else array.ndim - 2
        shape = list(array.shape)
        plan.append((kind, shape[axis]))
        shape[axis] *= n
        shapes.append(jax.ShapeDtypeStruct(tuple(shape), array.dtype))
        rows = array.shape[-2] // cut
        units += [(i, c * rows, rows) for c in range(cut)]
        moved += math.prod(shape) * 2
    return pl.pallas_call(
        functools.partial(ring_kernel, n, tuple(plan), tuple(units), len(after)),
        out_shape=shapes,
        in_specs=[pl.BlockSpec(memory_space=pl.ANY)] * (len(arrays) + len(after)),
        out_specs=[pl.BlockSpec(memory_space=pl.ANY)] * len(arrays),
        scratch_shapes=[
            pltpu.SemaphoreType.DMA((len(units), 2, n // 2)),
            pltpu.SemaphoreType.DMA((len(units), 2, n // 2)),
            pltpu.SemaphoreType.DMA((len(arrays),)),
        ],
        compiler_params=pltpu.CompilerParams(collective_id=collective_id, has_side_effects=True),
        cost_estimate=pl.CostEstimate(flops=0, bytes_accessed=moved * 12, transcendentals=0),
        name="ring_gather",
    )(*arrays, *after)


def on_device(
    tokens,
    grid_sides,
    offsets,
    merge_rows,
    routes,
    norm_gain,
    norm_bias,
    layer_scale,
    qkv_weight,
    out_weight,
    gate_up,
    down_weight,
    merge_gain,
    merge_bias,
    merge_weight,
):
    images = grid_sides.shape[0]
    row_count = min(tokens.shape[0], -(-images * (5 + GMAX * GMAX) // 16) * 16)
    all_tokens, tokens = tokens, tokens[:row_count]
    model_width = tokens.shape[1]
    groups = lax.axis_size("req")
    shards = lax.axis_size("mlp")
    member = lax.axis_index("mlp")
    piece_width = model_width // shards
    start_col = member * piece_width
    slot_count = merge_rows.shape[0]
    numbers = jnp.arange(grid_sides.shape[0], dtype=jnp.int32)
    image_id, tables = row_layout(grid_sides, offsets, row_count, HEAD)
    cos_y, sin_y, cos_x, sin_x = (table[:, 0] for table in tables)
    heads_here = qkv_weight.shape[1] // (3 * HEAD)
    queries, key_rows, values, out_all = norm_project(
        all_tokens,
        row_count,
        norm_gain[:1],
        norm_bias[:1],
        qkv_weight,
        out_weight,
        jnp.concatenate([cos_y, cos_y, cos_x, cos_x], axis=1),
        jnp.concatenate([-sin_y, sin_y, -sin_x, sin_x], axis=1),
    )
    attended, logits = attend(queries, key_rows, values, image_id, numbers)
    attended_flat = attended.reshape(row_count, heads_here * HEAD)
    head_terms = jnp.dot(
        attended_flat,
        out_all,
        preferred_element_type=jnp.float32,
    ).astype(jnp.bfloat16)
    gate_all, down_all = ring_gather(
        [gate_up, down_weight], ["mid", "col"], [2, 2], 1, after=(head_terms[:16, :128],)
    )
    attn_sum = lax.psum(head_terms, "mlp").astype(jnp.float32)
    residual = (tokens.astype(jnp.float32) + layer_scale[0] * attn_sum).astype(jnp.bfloat16)
    resid_piece = lax.dynamic_slice_in_dim(residual, start_col, piece_width, 1)
    normed_two = layer_norm(residual.astype(jnp.float32), norm_gain[1], norm_bias[1]).astype(
        jnp.bfloat16
    )
    columns = normed_two
    gate_pair = jnp.einsum(
        "rk,pkn->prn",
        columns,
        gate_all,
        preferred_element_type=jnp.float32,
    )
    hidden = (jax.nn.silu(gate_pair[0]) * gate_pair[1]).astype(jnp.bfloat16)
    hidden_terms = jnp.dot(hidden, down_all, preferred_element_type=jnp.float32)
    ffn_piece = lax.psum_scatter(
        hidden_terms.astype(jnp.bfloat16), "mlp", scatter_dimension=1, tiled=True
    ).astype(jnp.float32)
    own_scale_two = lax.dynamic_slice_in_dim(layer_scale[1], start_col, piece_width, 0)
    final_piece = (resid_piece.astype(jnp.float32) + own_scale_two * ffn_piece).astype(jnp.bfloat16)
    live = -(-(GMAX // 2) ** 2 // 8) * 8
    picked = merge_rows.reshape(images, MSLOT, 4)[:, :live].reshape(images * live, 4)
    merged = final_piece[picked].astype(jnp.float32)
    totals, squares = lax.psum(
        (jnp.sum(merged, axis=(1, 2)), jnp.sum(merged * merged, axis=(1, 2))), "mlp"
    )
    center = totals / (4 * model_width)
    spread = squares / (4 * model_width) - center * center
    scaled = (
        (merged - center[:, None, None]) * lax.rsqrt(spread + EPS)[:, None, None] * merge_gain[None]
        + merge_bias[None]
    )
    sent = images * live
    is_live = (
        jnp.arange(live, dtype=jnp.int32)[None, :]
        < (grid_sides[:, 0] // 2 * (grid_sides[:, 1] // 2))[:, None]
    ).reshape(sent)
    scaled = jnp.where(is_live[:, None, None], scaled, 0.0).astype(jnp.bfloat16)
    (scaled_all,) = ring_gather([scaled.reshape(sent, 4 * piece_width)], ["row"], [1], 2)
    merge_terms = jnp.dot(
        scaled_all,
        merge_weight.reshape(4 * piece_width, merge_weight.shape[2]),
        preferred_element_type=jnp.float32,
    ).astype(jnp.bfloat16)
    targets = routes[:, 0].reshape(groups, slot_count)
    earlier = jnp.arange(slot_count)[None, :] < jnp.arange(slot_count)[:, None]
    same = (targets[:, :, None] == targets[:, None, :]) & earlier[None]
    ranks = jnp.sum(same.astype(jnp.int32), axis=2)
    rows_out = groups * CAP
    dest = targets * rows_out + jnp.arange(groups, dtype=jnp.int32)[:, None] * CAP + ranks
    dest = dest.reshape(groups, images, MSLOT)[:, :, :live].reshape(groups * sent)
    chosen = (jnp.arange(groups * rows_out, dtype=jnp.int32)[:, None] == dest[None, :]).astype(
        jnp.bfloat16
    )
    placed_rows = jnp.dot(chosen, merge_terms, preferred_element_type=jnp.float32).astype(
        jnp.bfloat16
    )
    received = lax.all_to_all(
        placed_rows.reshape(groups, rows_out, merge_terms.shape[1]),
        "req",
        split_axis=0,
        concat_axis=0,
        tiled=True,
    )
    terms = lax.all_to_all(received, "mlp", split_axis=0, concat_axis=0, tiled=True)
    terms = terms.reshape(shards, groups // shards, rows_out, merge_terms.shape[1])
    embeds = jnp.sum(terms.astype(jnp.float32), axis=0).astype(jnp.bfloat16)
    embeds = embeds.transpose(1, 0, 2).reshape(rows_out, OUT // shards)
    row_squares = jnp.sum(jnp.square(embeds.astype(jnp.float32)), axis=1)
    total_squares = lax.psum(row_squares, "mlp")
    token_norms = jnp.sqrt(total_squares / OUT + EPS)
    return (embeds, token_norms, logits)


def solution(mesh):
    placed = (
        P("req", None),
        P("req", None),
        P("req"),
        P("req", None),
        P(),
        P(),
        P(),
        P(),
        P("req", "mlp"),
        P("mlp", "req"),
        P(None, "req", "mlp"),
        P("mlp", "req"),
        P(None, "mlp"),
        P(None, "mlp"),
        P(None, "mlp", "req"),
    )
    return jax.shard_map(
        on_device,
        mesh=mesh,
        in_specs=placed,
        out_specs=(P("req", "mlp"), P("req"), P("req", "mlp")),
        check_vma=False,
    )
```
